32 devices in a mesh: row: 8 (over y, x, core), col: 4 (over z).
Axes of the slice: x: 2, y: 2, z: 4, core: 2. Of those that a mesh axis runs over, the one named last changes fastest.
Arguments:
- features: float32 [1536, 256], P(('row', 'col')), may hold values from -6 to 6
- inv_scale: float32 [256], replicated, may hold values from 0.001953125 to 0.015625
- probe_u: float32 [1536, 64], P(('row', 'col')), may hold values from -6 to 6
- solve_v: float32 [1536, 64], P(('row', 'col')), may hold values from -6 to 6
Outputs:
- feature_grad: float32 [1536, 256], P(('row', 'col'))
The draws below stay inside these ranges and needn't reach their ends.
All inputs are finite; a program needn't handle non-finite values.
Results may differ from the reference program's by a relative error of at most 0.0003.
Values sent between devices are 32-bit elements; how exact they have to be, the bound alone decides.
A program may use at most 64 MiB of HBM per device.

```python
import math
import jax
import jax.numpy as jnp
from jax import lax

P_DEV = 48
F = 256
RANK = 64
N = 1536
N_COL = 4


def block_scale(key, dims, shards, least, largest):
    level, own = 1.0, jax.random.fold_in(key, 6)
    for dim, parts in shards:
        heights = jnp.exp(jax.random.uniform(jax.random.fold_in(own, dim), (parts,), jnp.float32, least / len(shards), largest / len(shards)))
        level = level * jnp.repeat(heights, dims[dim] // parts).reshape([-1 if axis == dim else 1 for axis in range(len(dims))])
    return level


def centred(key, dims, scale, most, cuts=(), kind=jnp.bfloat16):
    array = jax.random.normal(key, dims, jnp.float32) * scale
    if len(cuts) > 0:
        array = block_scale(key, dims, cuts, -0.22, 0.18) * array
    return jnp.clip(array, min=-most, max=most).astype(kind)


def setup_inputs(seed: int = 0) -> dict:
    key_of = jax.random.split(jax.random.key(seed), 5)
    features = centred(key_of[0], (N, F), 1.0, 6.0, ((0, 32),), jnp.float32)
    inv_scale = jnp.clip(jnp.exp(jax.random.uniform(key_of[1], (F,), jnp.float32, math.log(0.001953125), math.log(0.015625))), 0.001953125, 0.015625)
    probe_u = centred(key_of[2], (N, RANK), 1.0, 6.0, ((0, 32),), jnp.float32)
    solve_v = centred(key_of[3], (N, RANK), 1.0, 6.0, ((0, 32),), jnp.float32)
    return {"features": features, "inv_scale": inv_scale, "probe_u": probe_u, "solve_v": solve_v}


def reference(features, inv_scale, probe_u, solve_v):
    block_rows = P_DEV * N_COL
    blocks_count = features.shape[0] // block_rows
    scaled = features * inv_scale
    squares = jnp.sum(scaled * features, axis=1)
    left_all = jnp.concatenate([probe_u, solve_v], axis=1)
    right_all = jnp.concatenate([solve_v, probe_u], axis=1)

    def row_block(index):
        offset = (index * block_rows).astype(jnp.int32)
        row_x = lax.dynamic_slice_in_dim(features, offset, block_rows, 0)
        row_left = lax.dynamic_slice_in_dim(left_all, offset, block_rows, 0)
        row_sq = lax.dynamic_slice_in_dim(squares, offset, block_rows, 0)
        inner_prod = jnp.dot(row_x, scaled.T, precision=lax.Precision.HIGHEST, preferred_element_type=jnp.float32)
        distance = row_sq[:, None] + squares[None, :] - 2.0 * inner_prod
        kernel = jnp.exp(-0.5 * distance)
        mixing = jnp.dot(row_left, right_all.T, precision=lax.Precision.HIGHEST, preferred_element_type=jnp.float32)
        coupling = mixing * kernel
        pulled = jnp.dot(coupling, features, precision=lax.Precision.HIGHEST, preferred_element_type=jnp.float32)
        row_sums = jnp.sum(coupling, axis=1)
        return (pulled - row_sums[:, None] * row_x) * inv_scale

    result = lax.map(row_block, jnp.arange(blocks_count, dtype=jnp.int32))
    return result.reshape(features.shape[0], features.shape[1])
```

```python
import functools
import math

import jax
import jax.numpy as jnp
from jax import lax
from jax.experimental import pallas as pl
from jax.experimental.pallas import tpu as pltpu
from jax.sharding import PartitionSpec as P

MESH = pl.DeviceIdType.MESH
LAST = (((1,), (1,)), ((), ()))


def split(count):
    return max(part for part in range(1, math.isqrt(count) + 1) if count % part == 0)


def exact_dot(left, right, dims):
    return lax.dot_general(
        left, right, dims, precision=lax.Precision.HIGHEST, preferred_element_type=jnp.float32
    )


def kernel(
    sizes,
    x_ref,
    scale_ref,
    u_ref,
    v_ref,
    out_ref,
    row_buf,
    col_buf,
    part,
    landed,
    scale_buf,
    u_buf,
    v_buf,
    local_sem,
    row_send,
    row_recv,
    col_send,
    col_recv,
    twin_send,
    twin_recv,
    red_send,
    red_recv,
):
    n_core, n_a, n_b, n_c, n_d = sizes
    points, width = x_ref.shape
    rank = u_ref.shape[1]
    row, col = lax.axis_index("row"), lax.axis_index("col")
    core, chip = lax.rem(row, n_core), lax.div(row, n_core)
    a, c = lax.rem(chip, n_a), lax.div(chip, n_a)
    b, d = lax.rem(col, n_b), lax.div(col, n_b)

    def device(da=0, db=0, dc=0, dd=0, dcore=0):
        to_chip = lax.rem(c + dc, n_c) * n_a + lax.rem(a + da, n_a)
        to_row = to_chip * n_core + lax.rem(core + dcore, n_core)
        return (to_row, lax.rem(d + dd, n_d) * n_b + lax.rem(b + db, n_b))

    def row_slot(da, db):
        return da * n_b + db

    def col_slot(dc, dd):
        return dc * n_d + dd

    n_row, n_col = n_a * n_b, n_c * n_d
    peers = [device(da=i, db=j) for i in range(n_a) for j in range(n_b) if i + j > 0]
    peers += [device(dc=i) for i in range(1, n_c)]
    peers += [device(dd=i) for i in range(1, n_d)]
    peers += [device(dcore=i) for i in range(1, n_core)]
    barrier = pltpu.get_barrier_semaphore()
    for peer in peers:
        pl.semaphore_signal(barrier, inc=1, device_id=peer, device_id_type=MESH)

    loads = [
        pltpu.make_async_copy(x_ref, row_buf.at[0, :, pl.ds(0, width)], local_sem.at[0]),
        pltpu.make_async_copy(u_ref, u_buf, local_sem.at[1]),
        pltpu.make_async_copy(v_ref, v_buf, local_sem.at[2]),
        pltpu.make_async_copy(scale_ref, scale_buf, local_sem.at[3]),
    ]
    for load in loads:
        load.start()
    for load in loads:
        load.wait()
    row_buf[0, :, width:] = jnp.concatenate([u_buf[...], v_buf[...]], axis=1)
    col_buf[0] = row_buf[0]
    pl.semaphore_wait(barrier, len(peers))

    def remote(src, dst, send, recv, to):
        return pltpu.make_async_remote_copy(
            src_ref=src, dst_ref=dst, send_sem=send, recv_sem=recv, device_id=to, device_id_type=MESH
        )

    def row_copy(src, dst, **step):
        back = {name: {"da": n_a, "db": n_b}[name] - by for name, by in step.items()}
        return remote(
            row_buf.at[src], row_buf.at[dst], row_send.at[dst], row_recv.at[dst], device(**back)
        )

    def col_copy(src, dst, **step):
        back = {name: {"dc": n_c, "dd": n_d}[name] - by for name, by in step.items()}
        return remote(
            col_buf.at[src], col_buf.at[dst], col_send.at[dst], col_recv.at[dst], device(**back)
        )

    def twin_copy(slot):
        return remote(
            col_buf.at[slot],
            col_buf.at[n_col + slot],
            twin_send.at[slot],
            twin_recv.at[slot],
            device(dcore=1),
        )

    near = [row_copy(0, row_slot(0, j), db=j) for j in range(1, n_b)]
    far = [col_copy(0, col_slot(0, j), dd=j) for j in range(1, n_d)]
    side = [
        [row_copy(row_slot(0, j), row_slot(i, j), da=i) for i in range(1, n_a)] for j in range(n_b)
    ]
    over = [
        [col_copy(col_slot(0, j), col_slot(i, j), dc=i) for i in range(1, n_c)] for j in range(n_d)
    ]
    twin = [twin_copy(slot) for slot in range(n_col)] if n_core > 1 else []

    def start(copies):
        for copy in copies:
            copy.start()

    start(far)
    start(near)
    start(over[0])
    start(side[0])
    start(twin[:1])
    for j, copy in enumerate(near, 1):
        copy.wait_recv()
        start(side[j])
    for j, copy in enumerate(far, 1):
        copy.wait_recv()
        start(over[j])
        start(twin[j : j + 1])
    for j in range(n_d):
        for i, copy in enumerate(over[j], 1):
            copy.wait_recv()
            start(twin[col_slot(i, j) : col_slot(i, j) + 1])
    for copies in side:
        for copy in copies:
            copy.wait_recv()
    for copy in twin:
        copy.wait_recv()

    scale = scale_buf[...].reshape(1, width)
    cols = col_buf[...].reshape(n_core * n_col * points, width + 2 * rank)
    col_x, col_uv = cols[:, :width], cols[:, width:]
    col_scaled = col_x * scale
    col_sq = exact_dot(jnp.ones((8, width), jnp.float32), col_scaled * col_x, LAST)[:1]
    reduces = []

    def tile(first, last):
        rows = row_buf[first:last].reshape((last - first) * points, width + 2 * rank)
        row_x, row_uv = rows[:, :width], rows[:, width:]
        row_vu = jnp.concatenate([row_uv[:, rank:], row_uv[:, :rank]], axis=1)
        row_sq = jnp.sum(row_x * scale * row_x, axis=1, keepdims=True)
        inner = exact_dot(row_x, col_scaled, LAST)
        mixing = exact_dot(row_vu, col_uv, LAST)
        coupling = mixing * jnp.exp(-0.5 * (row_sq + col_sq - 2.0 * inner))
        pulled = exact_dot(coupling, col_x, (((1,), (0,)), ((), ())))
        term = pulled - jnp.sum(coupling, axis=1, keepdims=True) * row_x
        part[first:last] = term.reshape(last - first, points, width)

    if n_row > 1:
        step = 3
        for first in range(1, n_row, step):
            tile(first, min(first + step, n_row))
            for slot in range(first, min(first + step, n_row)):
                i, j = slot // n_b, slot % n_b
                copy = remote(
                    part.at[slot],
                    landed.at[slot],
                    red_send.at[slot],
                    red_recv.at[slot],
                    device(da=i, db=j),
                )
                copy.start()
                reduces.append(copy)
    tile(0, 1)
    total = part[0]
    for slot, copy in enumerate(reduces, 1):
        copy.wait_recv()
        total = total + landed[slot]
    out_ref[...] = total * scale

    for copies in (near, far, *side, *over, twin, reduces):
        for copy in copies:
            copy.wait_send()


def on_device(sizes, features, inv_scale, probe_u, solve_v):
    n_core, n_a, n_b, n_c, n_d = sizes
    points, width = features.shape
    rank = probe_u.shape[1]
    n_row, n_col = n_a * n_b, n_c * n_d
    f32, dma = jnp.float32, pltpu.SemaphoreType.DMA
    return pl.pallas_call(
        functools.partial(kernel, sizes),
        out_shape=jax.ShapeDtypeStruct((points, width), f32),
        in_specs=[pl.BlockSpec(memory_space=pl.ANY)] * 4,
        out_specs=pl.BlockSpec(memory_space=pltpu.VMEM),
        scratch_shapes=[
            pltpu.VMEM((n_row, points, width + 2 * rank), f32),
            pltpu.VMEM((n_core * n_col, points, width + 2 * rank), f32),
            pltpu.VMEM((n_row, points, width), f32),
            pltpu.VMEM((n_row, points, width), f32),
            pltpu.VMEM((width,), f32),
            pltpu.VMEM((points, rank), f32),
            pltpu.VMEM((points, rank), f32),
            dma((4,)),
            dma((n_row,)),
            dma((n_row,)),
            dma((n_col,)),
            dma((n_col,)),
            dma((n_col,)),
            dma((n_col,)),
            dma((n_row,)),
            dma((n_row,)),
        ],
        compiler_params=pltpu.CompilerParams(
            collective_id=0, has_side_effects=True, vmem_limit_bytes=48 * 2**20
        ),
    )(features, inv_scale, probe_u, solve_v)


def solution(mesh):
    rows, cols = mesh.shape["row"], mesh.shape["col"]
    n_core = 2 if rows % 2 == 0 else 1
    chips = rows // n_core
    n_a, n_b = split(chips), split(cols)
    sizes = (n_core, n_a, n_b, chips // n_a, cols // n_b)
    return jax.shard_map(
        functools.partial(on_device, sizes),
        mesh=mesh,
        in_specs=(P(("row", "col"), None), P(), P(("row", "col"), None), P(("row", "col"), None)),
        out_specs=P(("row", "col"), None),
        check_vma=False,
    )
```

```python
import functools
import math

import jax
import jax.numpy as jnp
from jax import lax
from jax.experimental import pallas as pl
from jax.experimental.pallas import tpu as pltpu
from jax.sharding import PartitionSpec as P

MESH = pl.DeviceIdType.MESH
LAST = (((1,), (1,)), ((), ()))
FIRST = (((1,), (0,)), ((), ()))


def split(count):
    return max(part for part in range(1, math.isqrt(count) + 1) if count % part == 0)


def dot(left, right, dims):
    return lax.dot_general(left, right, dims, preferred_element_type=jnp.float32)


def halves(value):
    hi = value.astype(jnp.bfloat16)
    return hi, (value - hi.astype(jnp.float32)).astype(jnp.bfloat16)


def ends(square, side):
    lane = lax.broadcasted_iota(jnp.int32, (square.shape[0], 128), 1)
    rest, lanes = -0.5 * square, jnp.where(lane < 6, 1.0, 0.0)
    for index in range(3):
        piece = rest.astype(jnp.bfloat16).astype(jnp.float32)
        lanes = jnp.where(lane == 3 * side + index, piece, lanes)
        rest = rest - piece
    return lanes.astype(jnp.bfloat16)


def kernel(
    sizes,
    x_ref,
    scale_ref,
    u_ref,
    v_ref,
    out_ref,
    row_buf,
    col_buf,
    part,
    landed,
    scale_buf,
    u_buf,
    v_buf,
    local_sem,
    row_send,
    row_recv,
    col_send,
    col_recv,
    twin_send,
    twin_recv,
    red_send,
    red_recv,
):
    n_core, n_a, n_b, n_c, n_d = sizes
    points, width = x_ref.shape
    rank = u_ref.shape[1]
    row, col = lax.axis_index("row"), lax.axis_index("col")
    core, chip = lax.rem(row, n_core), lax.div(row, n_core)
    a, c = lax.rem(chip, n_a), lax.div(chip, n_a)
    b, d = lax.rem(col, n_b), lax.div(col, n_b)

    def device(da=0, db=0, dc=0, dd=0, dcore=0):
        to_chip = lax.rem(c + dc, n_c) * n_a + lax.rem(a + da, n_a)
        to_row = to_chip * n_core + lax.rem(core + dcore, n_core)
        return (to_row, lax.rem(d + dd, n_d) * n_b + lax.rem(b + db, n_b))

    def row_slot(da, db):
        return da * n_b + db

    def col_slot(dc, dd):
        return dc * n_d + dd

    n_row, n_col = n_a * n_b, n_c * n_d
    peers = [device(da=i, db=j) for i in range(n_a) for j in range(n_b) if i + j > 0]
    peers += [device(dc=i) for i in range(1, n_c)]
    peers += [device(dd=i) for i in range(1, n_d)]
    peers += [device(dcore=i) for i in range(1, n_core)]
    barrier = pltpu.get_barrier_semaphore()
    for peer in peers:
        pl.semaphore_signal(barrier, inc=1, device_id=peer, device_id_type=MESH)

    loads = [
        pltpu.make_async_copy(x_ref, row_buf.at[0, :, pl.ds(0, width)], local_sem.at[0]),
        pltpu.make_async_copy(u_ref, u_buf, local_sem.at[1]),
        pltpu.make_async_copy(v_ref, v_buf, local_sem.at[2]),
        pltpu.make_async_copy(scale_ref, scale_buf, local_sem.at[3]),
    ]
    for load in loads:
        load.start()
    for load in loads:
        load.wait()
    row_buf[0, :, width:] = jnp.concatenate([u_buf[...], v_buf[...]], axis=1)
    col_buf[0] = row_buf[0]
    pl.semaphore_wait(barrier, len(peers))

    def remote(src, dst, send, recv, to):
        return pltpu.make_async_remote_copy(
            src_ref=src, dst_ref=dst, send_sem=send, recv_sem=recv, device_id=to, device_id_type=MESH
        )

    def row_copy(src, dst, **step):
        back = {name: {"da": n_a, "db": n_b}[name] - by for name, by in step.items()}
        return remote(
            row_buf.at[src], row_buf.at[dst], row_send.at[dst], row_recv.at[dst], device(**back)
        )

    def col_copy(src, dst, **step):
        back = {name: {"dc": n_c, "dd": n_d}[name] - by for name, by in step.items()}
        return remote(
            col_buf.at[src], col_buf.at[dst], col_send.at[dst], col_recv.at[dst], device(**back)
        )

    def twin_copy(slot):
        return remote(
            col_buf.at[slot],
            col_buf.at[n_col + slot],
            twin_send.at[slot],
            twin_recv.at[slot],
            device(dcore=1),
        )

    near = [row_copy(0, row_slot(0, j), db=j) for j in range(1, n_b)]
    far = [col_copy(0, col_slot(0, j), dd=j) for j in range(1, n_d)]
    side = [
        [row_copy(row_slot(0, j), row_slot(i, j), da=i) for i in range(1, n_a)] for j in range(n_b)
    ]
    over = [
        [col_copy(col_slot(0, j), col_slot(i, j), dc=i) for i in range(1, n_c)] for j in range(n_d)
    ]
    twin = [twin_copy(slot) for slot in range(n_col)] if n_core > 1 else []

    def start(copies):
        for copy in copies:
            copy.start()

    start(far)
    start(near)
    start(over[0])
    start(side[0])
    start(twin[:1])
    for j, copy in enumerate(near, 1):
        copy.wait_recv()
        start(side[j])
    for j, copy in enumerate(far, 1):
        copy.wait_recv()
        start(over[j])
        start(twin[j : j + 1])
    for j in range(n_d):
        for i, copy in enumerate(over[j], 1):
            copy.wait_recv()
            start(twin[col_slot(i, j) : col_slot(i, j) + 1])
    for copies in side:
        for copy in copies:
            copy.wait_recv()

    scale = scale_buf[...].reshape(1, width)
    rows = row_buf[...].reshape(n_row * points, width + 2 * rank)
    row_x, row_uv = rows[:, :width], rows[:, width:]
    row_sq = jnp.sum(row_x * scale * row_x, axis=1, keepdims=True)
    row_x_hi, row_x_lo = halves(row_x)
    row_left = jnp.concatenate([row_x_hi, row_x_lo, row_x_hi, ends(row_sq, 1)], axis=1)
    vu_hi, vu_lo = halves(jnp.concatenate([row_uv[:, rank:], row_uv[:, :rank]], axis=1))
    vu_left = jnp.concatenate([vu_hi, vu_lo, vu_hi], axis=1)

    def chunk(core_slot):
        cols = col_buf[core_slot * n_col : (core_slot + 1) * n_col]
        cols = cols.reshape(n_col * points, width + 2 * rank)
        col_x = cols[:, :width]
        col_scaled = col_x * scale
        col_sq = jnp.sum(col_scaled * col_x, axis=1, keepdims=True)
        scaled_hi, scaled_lo = halves(col_scaled)
        col_right = jnp.concatenate([scaled_hi, scaled_hi, scaled_lo, ends(col_sq, 0)], axis=1)
        uv_hi, uv_lo = halves(cols[:, width:])
        uv_right = jnp.concatenate([uv_hi, uv_hi, uv_lo], axis=1)
        coupling = dot(vu_left, uv_right, LAST) * jnp.exp(dot(row_left, col_right, LAST))
        hi, lo = halves(coupling)
        col_x_hi, col_x_lo = halves(col_x)
        both = dot(jnp.concatenate([hi, lo], axis=0), col_x_hi, FIRST)
        pulled = both[: n_row * points] + both[n_row * points :] + dot(hi, col_x_lo, FIRST)
        return coupling, pulled, jnp.sum(coupling, axis=1, keepdims=True)

    coupling, pulled, sums = chunk(0)
    place = [lax.broadcasted_iota(jnp.int32, (points, n_col * points), axis) for axis in (0, 1)]
    diagonal = jnp.where(place[0] == place[1], coupling[:points], 0.0)
    diagonal = jnp.sum(diagonal, axis=1, keepdims=True)
    diag_hi, diag_lo = (half.astype(jnp.float32) for half in halves(diagonal))
    own = row_x[:points]
    own_hi, own_lo = (half.astype(jnp.float32) for half in halves(own))
    rest = diagonal * own - diag_hi * own_hi - diag_hi * own_lo - diag_lo * own_hi

    for copy in twin:
        copy.wait_recv()
    for core_slot in range(1, n_core):
        _, more_pulled, more_sums = chunk(core_slot)
        pulled, sums = pulled + more_pulled, sums + more_sums
    part[...] = (pulled - sums * row_x).reshape(n_row, points, width)

    reduces = []
    for slot in range(1, n_row):
        copy = remote(
            part.at[slot],
            landed.at[slot],
            red_send.at[slot],
            red_recv.at[slot],
            device(da=slot // n_b, db=slot % n_b),
        )
        copy.start()
        reduces.append(copy)
    total = part[0] + rest
    for slot, copy in enumerate(reduces, 1):
        copy.wait_recv()
        total = total + landed[slot]
    out_ref[...] = total * scale

    for copies in (near, far, *side, *over, twin, reduces):
        for copy in copies:
            copy.wait_send()


def on_device(sizes, features, inv_scale, probe_u, solve_v):
    n_core, n_a, n_b, n_c, n_d = sizes
    points, width = features.shape
    rank = probe_u.shape[1]
    n_row, n_col = n_a * n_b, n_c * n_d
    f32, dma = jnp.float32, pltpu.SemaphoreType.DMA
    return pl.pallas_call(
        functools.partial(kernel, sizes),
        out_shape=jax.ShapeDtypeStruct((points, width), f32),
        in_specs=[pl.BlockSpec(memory_space=pltpu.HBM)] * 4,
        out_specs=pl.BlockSpec(memory_space=pltpu.VMEM),
        scratch_shapes=[
            pltpu.VMEM((n_row, points, width + 2 * rank), f32),
            pltpu.VMEM((n_core * n_col, points, width + 2 * rank), f32),
            pltpu.VMEM((n_row, points, width), f32),
            pltpu.VMEM((n_row, points, width), f32),
            pltpu.VMEM((width,), f32),
            pltpu.VMEM((points, rank), f32),
            pltpu.VMEM((points, rank), f32),
            dma((4,)),
            dma((n_row,)),
            dma((n_row,)),
            dma((n_col,)),
            dma((n_col,)),
            dma((n_col,)),
            dma((n_col,)),
            dma((n_row,)),
            dma((n_row,)),
        ],
        compiler_params=pltpu.CompilerParams(
            collective_id=0, has_side_effects=True, vmem_limit_bytes=60 * 2**20
        ),
    )(features, inv_scale, probe_u, solve_v)


def solution(mesh):
    rows, cols = mesh.shape["row"], mesh.shape["col"]
    n_core = 2 if rows % 2 == 0 else 1
    chips = rows // n_core
    n_a, n_b = split(chips), split(cols)
    sizes = (n_core, n_a, n_b, chips // n_a, cols // n_b)
    return jax.shard_map(
        functools.partial(on_device, sizes),
        mesh=mesh,
        in_specs=(P(("row", "col"), None), P(), P(("row", "col"), None), P(("row", "col"), None)),
        out_specs=P(("row", "col"), None),
        check_vma=False,
    )
```

```python
import functools
import math

import jax
import jax.numpy as jnp
from jax import lax
from jax.experimental import pallas as pl
from jax.experimental.pallas import tpu as pltpu
from jax.sharding import PartitionSpec as P

MESH = pl.DeviceIdType.MESH
LAST = (((1,), (1,)), ((), ()))
FIRST = (((1,), (0,)), ((), ()))


def split(count):
    return max(part for part in range(1, math.isqrt(count) + 1) if count % part == 0)


def dot(left, right, dims):
    return lax.dot_general(left, right, dims, preferred_element_type=jnp.float32)


def halves(value):
    hi = value.astype(jnp.bfloat16)
    return hi, (value - hi.astype(jnp.float32)).astype(jnp.bfloat16)


def ends(square, side):
    lane = lax.broadcasted_iota(jnp.int32, (square.shape[0], 128), 1)
    rest, lanes = -0.5 * square, jnp.where(lane < 6, 1.0, 0.0)
    for index in range(3):
        piece = rest.astype(jnp.bfloat16).astype(jnp.float32)
        lanes = jnp.where(lane == 3 * side + index, piece, lanes)
        rest = rest - piece
    return lanes.astype(jnp.bfloat16)


def kernel(
    sizes,
    block_ref,
    scale_ref,
    out_ref,
    row_buf,
    col_buf,
    part,
    landed,
    row_send,
    row_recv,
    col_send,
    col_recv,
    twin_send,
    twin_recv,
    red_send,
    red_recv,
):
    n_core, n_a, n_b, n_c, n_d = sizes
    points, width = out_ref.shape
    rank = (block_ref.shape[1] - width) // 2
    row, col = lax.axis_index("row"), lax.axis_index("col")
    core, chip = lax.rem(row, n_core), lax.div(row, n_core)
    a, c = lax.rem(chip, n_a), lax.div(chip, n_a)
    b, d = lax.rem(col, n_b), lax.div(col, n_b)

    def device(da=0, db=0, dc=0, dd=0, dcore=0):
        to_chip = lax.rem(c + dc, n_c) * n_a + lax.rem(a + da, n_a)
        to_row = to_chip * n_core + lax.rem(core + dcore, n_core)
        return (to_row, lax.rem(d + dd, n_d) * n_b + lax.rem(b + db, n_b))

    def row_slot(da, db):
        return da * n_b + db

    def col_slot(dc, dd):
        return dc * n_d + dd

    n_row, n_col = n_a * n_b, n_c * n_d
    peers = [device(da=i, db=j) for i in range(n_a) for j in range(n_b) if i + j > 0]
    peers += [device(dc=i) for i in range(1, n_c)]
    peers += [device(dd=i) for i in range(1, n_d)]
    peers += [device(dcore=i) for i in range(1, n_core)]
    barrier = pltpu.get_barrier_semaphore()
    for peer in peers:
        pl.semaphore_signal(barrier, inc=1, device_id=peer, device_id_type=MESH)

    row_buf[0] = block_ref[...]
    col_buf[0] = block_ref[...]
    pl.semaphore_wait(barrier, len(peers))

    def remote(src, dst, send, recv, to):
        return pltpu.make_async_remote_copy(
            src_ref=src, dst_ref=dst, send_sem=send, recv_sem=recv, device_id=to, device_id_type=MESH
        )

    def row_copy(src, dst, **step):
        back = {name: {"da": n_a, "db": n_b}[name] - by for name, by in step.items()}
        return remote(
            row_buf.at[src], row_buf.at[dst], row_send.at[dst], row_recv.at[dst], device(**back)
        )

    def col_copy(src, dst, **step):
        back = {name: {"dc": n_c, "dd": n_d}[name] - by for name, by in step.items()}
        return remote(
            col_buf.at[src], col_buf.at[dst], col_send.at[dst], col_recv.at[dst], device(**back)
        )

    def twin_copy(slot):
        return remote(
            col_buf.at[slot],
            col_buf.at[n_col + slot],
            twin_send.at[slot],
            twin_recv.at[slot],
            device(dcore=1),
        )

    near = [row_copy(0, row_slot(0, j), db=j) for j in range(1, n_b)]
    far = [col_copy(0, col_slot(0, j), dd=j) for j in range(1, n_d)]
    side = [
        [row_copy(row_slot(0, j), row_slot(i, j), da=i) for i in range(1, n_a)] for j in range(n_b)
    ]
    over = [
        [col_copy(col_slot(0, j), col_slot(i, j), dc=i) for i in range(1, n_c)] for j in range(n_d)
    ]
    twin = [twin_copy(slot) for slot in range(n_col)] if n_core > 1 else []

    def start(copies):
        for copy in copies:
            copy.start()

    start(far)
    start(near)
    start(over[0])
    start(side[0])
    start(twin[:1])
    for j, copy in enumerate(near, 1):
        copy.wait_recv()
        start(side[j])
    for j, copy in enumerate(far, 1):
        copy.wait_recv()
        start(over[j])
        start(twin[j : j + 1])
    for j in range(n_d):
        for i, copy in enumerate(over[j], 1):
            copy.wait_recv()
            start(twin[col_slot(i, j) : col_slot(i, j) + 1])
    for copies in side:
        for copy in copies:
            copy.wait_recv()

    scale = scale_ref[...].reshape(1, width)
    rows = row_buf[...].reshape(n_row * points, width + 2 * rank)
    row_x, row_uv = rows[:, :width], rows[:, width:]
    row_sq = jnp.sum(row_x * scale * row_x, axis=1, keepdims=True)
    row_x_hi, row_x_lo = halves(row_x)
    row_left = jnp.concatenate([row_x_hi, row_x_lo, row_x_hi, ends(row_sq, 1)], axis=1)
    vu_hi, vu_lo = halves(jnp.concatenate([row_uv[:, rank:], row_uv[:, :rank]], axis=1))
    vu_left = jnp.concatenate([vu_hi, vu_lo, vu_hi], axis=1)

    def chunk(core_slot):
        cols = col_buf[core_slot * n_col : (core_slot + 1) * n_col]
        cols = cols.reshape(n_col * points, width + 2 * rank)
        col_x = cols[:, :width]
        col_scaled = col_x * scale
        col_sq = jnp.sum(col_scaled * col_x, axis=1, keepdims=True)
        scaled_hi, scaled_lo = halves(col_scaled)
        col_right = jnp.concatenate([scaled_hi, scaled_hi, scaled_lo, ends(col_sq, 0)], axis=1)
        uv_hi, uv_lo = halves(cols[:, width:])
        uv_right = jnp.concatenate([uv_hi, uv_hi, uv_lo], axis=1)
        coupling = dot(vu_left, uv_right, LAST) * jnp.exp(dot(row_left, col_right, LAST))
        hi, lo = halves(coupling)
        col_x_hi, col_x_lo = halves(col_x)
        both = dot(jnp.concatenate([hi, lo], axis=0), col_x_hi, FIRST)
        pulled = both[: n_row * points] + both[n_row * points :] + dot(hi, col_x_lo, FIRST)
        return coupling, pulled, jnp.sum(coupling, axis=1, keepdims=True)

    coupling, pulled, sums = chunk(0)
    place = [lax.broadcasted_iota(jnp.int32, (points, n_col * points), axis) for axis in (0, 1)]
    diagonal = jnp.where(place[0] == place[1], coupling[:points], 0.0)
    diagonal = jnp.sum(diagonal, axis=1, keepdims=True)
    diag_hi, diag_lo = (half.astype(jnp.float32) for half in halves(diagonal))
    own = row_x[:points]
    own_hi, own_lo = (half.astype(jnp.float32) for half in halves(own))
    rest = diagonal * own - diag_hi * own_hi - diag_hi * own_lo - diag_lo * own_hi

    for copy in twin:
        copy.wait_recv()
    for core_slot in range(1, n_core):
        _, more_pulled, more_sums = chunk(core_slot)
        pulled, sums = pulled + more_pulled, sums + more_sums
    part[...] = (pulled - sums * row_x).reshape(n_row, points, width)

    reduces = []
    for slot in range(1, n_row):
        copy = remote(
            part.at[slot],
            landed.at[slot],
            red_send.at[slot],
            red_recv.at[slot],
            device(da=slot // n_b, db=slot % n_b),
        )
        copy.start()
        reduces.append(copy)
    total = part[0] + rest
    for slot, copy in enumerate(reduces, 1):
        copy.wait_recv()
        total = total + landed[slot]
    out_ref[...] = total * scale

    for copies in (near, far, *side, *over, twin, reduces):
        for copy in copies:
            copy.wait_send()


def on_device(sizes, features, inv_scale, probe_u, solve_v):
    n_core, n_a, n_b, n_c, n_d = sizes
    points, width = features.shape
    rank = probe_u.shape[1]
    n_row, n_col = n_a * n_b, n_c * n_d
    f32, dma = jnp.float32, pltpu.SemaphoreType.DMA
    return pl.pallas_call(
        functools.partial(kernel, sizes),
        out_shape=jax.ShapeDtypeStruct((points, width), f32),
        in_specs=[pl.BlockSpec(memory_space=pltpu.VMEM)] * 2,
        out_specs=pl.BlockSpec(memory_space=pltpu.VMEM),
        scratch_shapes=[
            pltpu.VMEM((n_row, points, width + 2 * rank), f32),
            pltpu.VMEM((n_core * n_col, points, width + 2 * rank), f32),
            pltpu.VMEM((n_row, points, width), f32),
            pltpu.VMEM((n_row, points, width), f32),
            dma((n_row,)),
            dma((n_row,)),
            dma((n_col,)),
            dma((n_col,)),
            dma((n_col,)),
            dma((n_col,)),
            dma((n_row,)),
            dma((n_row,)),
        ],
        compiler_params=pltpu.CompilerParams(
            collective_id=0, has_side_effects=True, vmem_limit_bytes=48 * 2**20
        ),
    )(jnp.concatenate([features, probe_u, solve_v], axis=1), inv_scale)


def solution(mesh):
    rows, cols = mesh.shape["row"], mesh.shape["col"]
    n_core = 2 if rows % 2 == 0 else 1
    chips = rows // n_core
    n_a, n_b = split(chips), split(cols)
    sizes = (n_core, n_a, n_b, chips // n_a, cols // n_b)
    return jax.shard_map(
        functools.partial(on_device, sizes),
        mesh=mesh,
        in_specs=(P(("row", "col"), None), P(), P(("row", "col"), None), P(("row", "col"), None)),
        out_specs=P(("row", "col"), None),
        check_vma=False,
    )
```

```python
import functools
import math

import jax
import jax.numpy as jnp
from jax import lax
from jax.experimental import pallas as pl
from jax.experimental.pallas import tpu as pltpu
from jax.sharding import PartitionSpec as P

MESH = pl.DeviceIdType.MESH
LAST = (((1,), (1,)), ((), ()))
FIRST = (((1,), (0,)), ((), ()))


def split(count):
    return max(part for part in range(1, math.isqrt(count) + 1) if count % part == 0)


def dot(left, right, dims):
    return lax.dot_general(left, right, dims, preferred_element_type=jnp.float32)


def halves(value):
    hi = value.astype(jnp.bfloat16)
    return hi, (value - hi.astype(jnp.float32)).astype(jnp.bfloat16)


def ends(square, side):
    lane = lax.broadcasted_iota(jnp.int32, (square.shape[0], 128), 1)
    rest, lanes = -0.5 * square, jnp.where(lane < 6, 1.0, 0.0)
    for index in range(3):
        piece = rest.astype(jnp.bfloat16).astype(jnp.float32)
        lanes = jnp.where(lane == 3 * side + index, piece, lanes)
        rest = rest - piece
    return lanes.astype(jnp.bfloat16)


def kernel(
    sizes,
    block_ref,
    scale_ref,
    out_ref,
    row_buf,
    col_buf,
    part,
    landed,
    row_send,
    row_recv,
    col_send,
    col_recv,
    twin_send,
    twin_recv,
    red_send,
    red_recv,
):
    n_core, n_a, n_b, n_c, n_d = sizes
    points, width = out_ref.shape
    rank = (block_ref.shape[1] - width) // 2
    row, col = lax.axis_index("row"), lax.axis_index("col")
    core, chip = lax.rem(row, n_core), lax.div(row, n_core)
    a, c = lax.rem(chip, n_a), lax.div(chip, n_a)
    b, d = lax.rem(col, n_b), lax.div(col, n_b)

    def device(da=0, db=0, dc=0, dd=0, dcore=0):
        to_chip = lax.rem(c + dc, n_c) * n_a + lax.rem(a + da, n_a)
        to_row = to_chip * n_core + lax.rem(core + dcore, n_core)
        return (to_row, lax.rem(d + dd, n_d) * n_b + lax.rem(b + db, n_b))

    order = [(0, 0)] + [(0, j) for j in range(1, n_b)] + [(i, 0) for i in range(1, n_a)]
    early = len(order)
    order += [(i, j) for i in range(1, n_a) for j in range(1, n_b)]

    def row_slot(da, db):
        return order.index((da, db))

    def col_slot(dc, dd):
        return dc * n_d + dd

    n_row, n_col = n_a * n_b, n_c * n_d
    peers = [device(da=i, db=j) for i in range(n_a) for j in range(n_b) if i + j > 0]
    peers += [device(dc=i) for i in range(1, n_c)]
    peers += [device(dd=i) for i in range(1, n_d)]
    peers += [device(dcore=i) for i in range(1, n_core)]
    barrier = pltpu.get_barrier_semaphore()
    for peer in peers:
        pl.semaphore_signal(barrier, inc=1, device_id=peer, device_id_type=MESH)

    pl.semaphore_wait(barrier, len(peers))

    def remote(src, dst, send, recv, to):
        return pltpu.make_async_remote_copy(
            src_ref=src, dst_ref=dst, send_sem=send, recv_sem=recv, device_id=to, device_id_type=MESH
        )

    pieces = row_send.shape[1]
    piece = points // pieces

    def in_pieces(src, dst, send, recv, to):
        cuts = [pl.ds(index * piece, piece) for index in range(pieces)]
        return [
            remote(src.at[cut], dst.at[cut], send.at[index], recv.at[index], to)
            for index, cut in enumerate(cuts)
        ]

    def row_copy(i, j, by):
        src = block_ref if (i, j) in ((by, 0), (0, by)) else row_buf.at[row_slot(0, j)]
        to = device(da=n_a - by) if i else device(db=n_b - by)
        dst = row_slot(i, j)
        return in_pieces(src, row_buf.at[dst], row_send.at[dst], row_recv.at[dst], to)

    def col_copy(i, j, by):
        src = block_ref if (i, j) in ((by, 0), (0, by)) else col_buf.at[col_slot(0, j)]
        to = device(dc=n_c - by) if i else device(dd=n_d - by)
        dst = col_slot(i, j)
        return in_pieces(src, col_buf.at[dst], col_send.at[dst], col_recv.at[dst], to)

    def twin_copy(slot):
        src = col_buf.at[slot] if slot else block_ref
        dst = col_buf.at[n_col + slot]
        return in_pieces(src, dst, twin_send.at[slot], twin_recv.at[slot], device(dcore=1))

    near = [row_copy(0, j, j) for j in range(1, n_b)]
    far = [col_copy(0, j, j) for j in range(1, n_d)]
    side = [[row_copy(i, j, i) for i in range(1, n_a)] for j in range(n_b)]
    over = [[col_copy(i, j, i) for i in range(1, n_c)] for j in range(n_d)]
    twin = [twin_copy(slot) for slot in range(n_col)] if n_core > 1 else []

    def start(copies, index):
        for copy in copies:
            copy[index].start()

    steps = range(pieces)
    for copies in (far, over[0], side[0], twin[:1], near):
        for index in steps:
            start(copies, index)
    row_buf[0] = block_ref[...]
    col_buf[0] = block_ref[...]

    def pass_far(index):
        for j, copy in enumerate(far, 1):
            copy[index].wait_recv()
            start(over[j], index)
            start(twin[j : j + 1], index)

    def pass_over(j, index):
        for i, copy in enumerate(over[j], 1):
            copy[index].wait_recv()
            start(twin[col_slot(i, j) : col_slot(i, j) + 1], index)

    for index in steps:
        pass_far(index)
        pass_over(0, index)
    for index in steps:
        for j, copy in enumerate(near, 1):
            copy[index].wait_recv()
            start(side[j], index)
        for j in range(1, n_d):
            pass_over(j, index)
    for copy in side[0]:
        for index in steps:
            copy[index].wait_recv()

    scale = scale_ref[...].reshape(1, width)

    def row_side(first, last):
        rows = row_buf[first:last].reshape((last - first) * points, width + 2 * rank)
        row_x, row_uv = rows[:, :width], rows[:, width:]
        row_sq = jnp.sum(row_x * scale * row_x, axis=1, keepdims=True)
        hi, lo = halves(row_x)
        left = jnp.concatenate([hi, lo, hi, ends(row_sq, 1)], axis=1)
        vu_hi, vu_lo = halves(jnp.concatenate([row_uv[:, rank:], row_uv[:, :rank]], axis=1))
        return row_x, left, jnp.concatenate([vu_hi, vu_lo, vu_hi], axis=1)

    def col_side(core_slot):
        cols = col_buf[core_slot * n_col : (core_slot + 1) * n_col]
        cols = cols.reshape(n_col * points, width + 2 * rank)
        col_x = cols[:, :width]
        col_scaled = col_x * scale
        col_sq = jnp.sum(col_scaled * col_x, axis=1, keepdims=True)
        hi, lo = halves(col_scaled)
        right = jnp.concatenate([hi, hi, lo, ends(col_sq, 0)], axis=1)
        uv_hi, uv_lo = halves(cols[:, width:])
        return halves(col_x), right, jnp.concatenate([uv_hi, uv_hi, uv_lo], axis=1)

    def tile(row_terms, col_terms):
        (_, left, vu_left), ((x_hi, x_lo), right, uv_right) = row_terms, col_terms
        coupling = dot(vu_left, uv_right, LAST) * jnp.exp(dot(left, right, LAST))
        hi, lo = halves(coupling)
        both = dot(jnp.concatenate([hi, lo], axis=0), x_hi, FIRST)
        count = left.shape[0]
        pulled = both[:count] + both[count:] + dot(hi, x_lo, FIRST)
        return coupling, pulled, jnp.sum(coupling, axis=1, keepdims=True)

    def finish(first, last, row_x, pulled, sums):
        part[first:last] = (pulled - sums * row_x).reshape(last - first, points, width)
        for slot in range(max(first, 1), last):
            i, j = order[slot]
            to = device(da=i, db=j)
            copy = remote(
                part.at[slot], landed.at[slot], red_send.at[slot], red_recv.at[slot], to
            )
            copy.start()
            reduces.append(copy)

    reduces = []
    row_terms = row_side(0, early)
    row_x = row_terms[0]
    col_terms = [col_side(0)]
    coupling, pulled, sums = tile(row_terms, col_terms[0])
    place = [lax.broadcasted_iota(jnp.int32, (points, n_col * points), axis) for axis in (0, 1)]
    diagonal = jnp.where(place[0] == place[1], coupling[:points], 0.0)
    diagonal = jnp.sum(diagonal, axis=1, keepdims=True)
    diag_hi, diag_lo = (half.astype(jnp.float32) for half in halves(diagonal))
    own = row_x[:points]
    own_hi, own_lo = (half.astype(jnp.float32) for half in halves(own))
    rest = diagonal * own - diag_hi * own_hi - diag_hi * own_lo - diag_lo * own_hi

    for copy in twin:
        for index in steps:
            copy[index].wait_recv()
    for core_slot in range(1, n_core):
        col_terms.append(col_side(core_slot))
        _, more_pulled, more_sums = tile(row_terms, col_terms[core_slot])
        pulled, sums = pulled + more_pulled, sums + more_sums
    finish(0, early, row_x, pulled, sums)

    if early < n_row:
        for copies in side[1:]:
            for copy in copies:
                for index in steps:
                    copy[index].wait_recv()
        row_terms = row_side(early, n_row)
        results = [tile(row_terms, terms) for terms in col_terms]
        finish(
            early,
            n_row,
            row_terms[0],
            sum(result[1] for result in results),
            sum(result[2] for result in results),
        )
    total = part[0] + rest
    for slot, copy in enumerate(reduces, 1):
        copy.wait_recv()
        total = total + landed[slot]
    out_ref[...] = total * scale

    for copies in (near, far, *side, *over, twin):
        for copy in copies:
            for index in steps:
                copy[index].wait_send()
    for copy in reduces:
        copy.wait_send()


def on_device(sizes, features, inv_scale, probe_u, solve_v):
    n_core, n_a, n_b, n_c, n_d = sizes
    points, width = features.shape
    rank = probe_u.shape[1]
    n_row, n_col = n_a * n_b, n_c * n_d
    pieces = 2 if points % 16 == 0 else 1
    f32, dma = jnp.float32, pltpu.SemaphoreType.DMA
    return pl.pallas_call(
        functools.partial(kernel, sizes),
        out_shape=jax.ShapeDtypeStruct((points, width), f32),
        in_specs=[pl.BlockSpec(memory_space=pltpu.VMEM)] * 2,
        out_specs=pl.BlockSpec(memory_space=pltpu.VMEM),
        scratch_shapes=[
            pltpu.VMEM((n_row, points, width + 2 * rank), f32),
            pltpu.VMEM((n_core * n_col, points, width + 2 * rank), f32),
            pltpu.VMEM((n_row, points, width), f32),
            pltpu.VMEM((n_row, points, width), f32),
            dma((n_row, pieces)),
            dma((n_row, pieces)),
            dma((n_col, pieces)),
            dma((n_col, pieces)),
            dma((n_col, pieces)),
            dma((n_col, pieces)),
            dma((n_row,)),
            dma((n_row,)),
        ],
        compiler_params=pltpu.CompilerParams(
            collective_id=0, has_side_effects=True, vmem_limit_bytes=48 * 2**20
        ),
    )(jnp.concatenate([features, probe_u, solve_v], axis=1), inv_scale)


def solution(mesh):
    rows, cols = mesh.shape["row"], mesh.shape["col"]
    n_core = 2 if rows % 2 == 0 else 1
    chips = rows // n_core
    n_a, n_b = split(chips), split(cols)
    sizes = (n_core, n_a, n_b, chips // n_a, cols // n_b)
    return jax.shard_map(
        functools.partial(on_device, sizes),
        mesh=mesh,
        in_specs=(P(("row", "col"), None), P(), P(("row", "col"), None), P(("row", "col"), None)),
        out_specs=P(("row", "col"), None),
        check_vma=False,
    )
```

```python
import functools
import math

import jax
import jax.numpy as jnp
from jax import lax
from jax.experimental import pallas as pl
from jax.experimental.pallas import tpu as pltpu
from jax.sharding import PartitionSpec as P

MESH = pl.DeviceIdType.MESH
LAST = (((1,), (1,)), ((), ()))
FIRST = (((1,), (0,)), ((), ()))


def split(count):
    return max(part for part in range(1, math.isqrt(count) + 1) if count % part == 0)


def dot(left, right, dims):
    return lax.dot_general(left, right, dims, preferred_element_type=jnp.float32)


def halves(value):
    hi = value.astype(jnp.bfloat16)
    return hi, (value - hi.astype(jnp.float32)).astype(jnp.bfloat16)


def ends(square, side):
    lane = lax.broadcasted_iota(jnp.int32, (square.shape[0], 128), 1)
    rest, lanes = -0.5 * square, jnp.where(lane < 6, 1.0, 0.0)
    for index in range(3):
        piece = rest.astype(jnp.bfloat16).astype(jnp.float32)
        lanes = jnp.where(lane == 3 * side + index, piece, lanes)
        rest = rest - piece
    return lanes.astype(jnp.bfloat16)


def kernel(
    sizes,
    block_ref,
    scale_ref,
    out_ref,
    row_buf,
    col_buf,
    part,
    landed,
    row_send,
    row_recv,
    col_send,
    col_recv,
    twin_send,
    twin_recv,
    red_send,
    red_recv,
):
    n_core, n_a, n_b, n_c, n_d = sizes
    points, width = out_ref.shape
    rank = (block_ref.shape[1] - width) // 2
    row, col = lax.axis_index("row"), lax.axis_index("col")
    core, chip = lax.rem(row, n_core), lax.div(row, n_core)
    a, c = lax.rem(chip, n_a), lax.div(chip, n_a)
    b, d = lax.rem(col, n_b), lax.div(col, n_b)

    def around(own, count):
        return [own] + [lax.rem(own + step, count) for step in range(1, count)]

    cores, cs = around(core, n_core), [n_a * n_core * at for at in around(c, n_c)]
    rows_at = [n_core * at for at in around(a, n_a)]
    bs, ds = around(b, n_b), [n_b * at for at in around(d, n_d)]

    def device(da=0, db=0, dc=0, dd=0, dcore=0):
        return (cs[dc] + rows_at[da] + cores[dcore], ds[dd] + bs[db])

    order = [(0, 0)] + [(0, j) for j in range(1, n_b)] + [(i, 0) for i in range(1, n_a)]
    early = len(order)
    order += [(i, j) for i in range(1, n_a) for j in range(1, n_b)]

    def row_slot(da, db):
        return order.index((da, db))

    def col_slot(dc, dd):
        return dc * n_d + dd

    n_row, n_col = n_a * n_b, n_c * n_d
    peers = [device(da=i, db=j) for i in range(n_a) for j in range(n_b) if i + j > 0]
    peers += [device(dc=i) for i in range(1, n_c)]
    peers += [device(dd=i) for i in range(1, n_d)]
    peers += [device(dcore=i) for i in range(1, n_core)]
    barrier = pltpu.get_barrier_semaphore()
    for peer in peers:
        pl.semaphore_signal(barrier, inc=1, device_id=peer, device_id_type=MESH)

    pl.semaphore_wait(barrier, len(peers))

    def remote(src, dst, send, recv, to):
        return pltpu.make_async_remote_copy(
            src_ref=src, dst_ref=dst, send_sem=send, recv_sem=recv, device_id=to, device_id_type=MESH
        )

    pieces = row_send.shape[1]

    def in_pieces(count, src, dst, send, recv, to):
        size = points // count
        cuts = [pl.ds(index * size, size) for index in range(count)]
        return [
            remote(src.at[cut], dst.at[cut], send.at[index], recv.at[index], to)
            for index, cut in enumerate(cuts)
        ]

    def row_copy(i, j, by):
        direct = j == 0
        src = block_ref if direct or i == 0 else row_buf.at[row_slot(0, j)]
        to = device(da=n_a - by) if i else device(db=n_b - by)
        dst, count = row_slot(i, j), 1 if direct else pieces
        return in_pieces(count, src, row_buf.at[dst], row_send.at[dst], row_recv.at[dst], to)

    def col_copy(i, j, by):
        direct = j == 0
        src = block_ref if direct or i == 0 else col_buf.at[col_slot(0, j)]
        to = device(dc=n_c - by) if i else device(dd=n_d - by)
        dst, count = col_slot(i, j), 1 if direct else pieces
        return in_pieces(count, src, col_buf.at[dst], col_send.at[dst], col_recv.at[dst], to)

    def twin_copy(slot):
        src = col_buf.at[slot] if slot else block_ref
        dst = col_buf.at[n_col + slot]
        return in_pieces(1, src, dst, twin_send.at[slot], twin_recv.at[slot], device(dcore=1))

    near = [row_copy(0, j, j) for j in range(1, n_b)]
    far = [col_copy(0, j, j) for j in range(1, n_d)]
    side = [[row_copy(i, j, i) for i in range(1, n_a)] for j in range(n_b)]
    over = [[col_copy(i, j, i) for i in range(1, n_c)] for j in range(n_d)]
    twin = [twin_copy(slot) for slot in range(n_col)] if n_core > 1 else []

    def start(copies):
        for copy in copies:
            copy.start()

    def arrive(copies):
        for copy in copies:
            copy.wait_recv()

    def start_twin(i, j):
        if n_core > 1:
            start(twin[col_slot(i, j)])

    for index in range(pieces):
        start([copy[index] for copy in far + near])
    for copy in over[0] + side[0] + twin[:1]:
        start(copy)
    row_buf[0] = block_ref[...]
    col_buf[0] = block_ref[...]

    for index in range(pieces):
        for j, copy in enumerate(far, 1):
            copy[index].wait_recv()
            start([relay[index] for relay in over[j]])
        for j, copy in enumerate(near, 1):
            copy[index].wait_recv()
            start([relay[index] for relay in side[j]])
    for j in range(1, n_d):
        start_twin(0, j)
    for j in range(n_d):
        for i, copy in enumerate(over[j], 1):
            arrive(copy)
            start_twin(i, j)
    for copy in side[0]:
        arrive(copy)

    scale = scale_ref[...].reshape(1, width)

    def row_side(first, last):
        rows = row_buf[first:last].reshape((last - first) * points, width + 2 * rank)
        row_x, row_uv = rows[:, :width], rows[:, width:]
        row_sq = jnp.sum(row_x * scale * row_x, axis=1, keepdims=True)
        hi, lo = halves(row_x)
        left = jnp.concatenate([hi, lo, hi, ends(row_sq, 1)], axis=1)
        vu_hi, vu_lo = halves(jnp.concatenate([row_uv[:, rank:], row_uv[:, :rank]], axis=1))
        return row_x, left, jnp.concatenate([vu_hi, vu_lo, vu_hi], axis=1)

    def col_side(core_slot):
        cols = col_buf[core_slot * n_col : (core_slot + 1) * n_col]
        cols = cols.reshape(n_col * points, width + 2 * rank)
        col_x = cols[:, :width]
        col_scaled = col_x * scale
        col_sq = jnp.sum(col_scaled * col_x, axis=1, keepdims=True)
        hi, lo = halves(col_scaled)
        right = jnp.concatenate([hi, hi, lo, ends(col_sq, 0)], axis=1)
        uv_hi, uv_lo = halves(cols[:, width:])
        return halves(col_x), right, jnp.concatenate([uv_hi, uv_hi, uv_lo], axis=1)

    def tile(row_terms, col_terms):
        (_, left, vu_left), ((x_hi, x_lo), right, uv_right) = row_terms, col_terms
        coupling = dot(vu_left, uv_right, LAST) * jnp.exp(dot(left, right, LAST))
        hi, lo = halves(coupling)
        both = dot(jnp.concatenate([hi, lo], axis=0), x_hi, FIRST)
        count = left.shape[0]
        pulled = both[:count] + both[count:] + dot(hi, x_lo, FIRST)
        return coupling, pulled, jnp.sum(coupling, axis=1, keepdims=True)

    def finish(first, last, row_x, pulled, sums):
        part[first:last] = (pulled - sums * row_x).reshape(last - first, points, width)
        for slot in range(max(first, 1), last):
            i, j = order[slot]
            to = device(da=i, db=j)
            copy = remote(
                part.at[slot], landed.at[slot], red_send.at[slot], red_recv.at[slot], to
            )
            copy.start()
            reduces.append(copy)

    reduces = []
    row_terms = row_side(0, early)
    row_x = row_terms[0]
    col_terms = [col_side(0)]
    coupling, pulled, sums = tile(row_terms, col_terms[0])
    place = [lax.broadcasted_iota(jnp.int32, (points, n_col * points), axis) for axis in (0, 1)]
    diagonal = jnp.where(place[0] == place[1], coupling[:points], 0.0)
    diagonal = jnp.sum(diagonal, axis=1, keepdims=True)
    diag_hi, diag_lo = (half.astype(jnp.float32) for half in halves(diagonal))
    own = row_x[:points]
    own_hi, own_lo = (half.astype(jnp.float32) for half in halves(own))
    rest = diagonal * own - diag_hi * own_hi - diag_hi * own_lo - diag_lo * own_hi

    for copy in twin:
        arrive(copy)
    for core_slot in range(1, n_core):
        col_terms.append(col_side(core_slot))
        _, more_pulled, more_sums = tile(row_terms, col_terms[core_slot])
        pulled, sums = pulled + more_pulled, sums + more_sums
    finish(0, early, row_x, pulled, sums)

    if early < n_row:
        for copies in side[1:]:
            for copy in copies:
                arrive(copy)
        row_terms = row_side(early, n_row)
        results = [tile(row_terms, terms) for terms in col_terms]
        finish(
            early,
            n_row,
            row_terms[0],
            sum(result[1] for result in results),
            sum(result[2] for result in results),
        )
    total = part[0] + rest
    for slot, copy in enumerate(reduces, 1):
        copy.wait_recv()
        total = total + landed[slot]
    out_ref[...] = total * scale

    for copies in (near, far, *side, *over, twin):
        for copy in copies:
            for part_copy in copy:
                part_copy.wait_send()
    for copy in reduces:
        copy.wait_send()


def on_device(sizes, features, inv_scale, probe_u, solve_v):
    n_core, n_a, n_b, n_c, n_d = sizes
    points, width = features.shape
    rank = probe_u.shape[1]
    n_row, n_col = n_a * n_b, n_c * n_d
    pieces = 2 if points % 16 == 0 else 1
    f32, dma = jnp.float32, pltpu.SemaphoreType.DMA
    return pl.pallas_call(
        functools.partial(kernel, sizes),
        out_shape=jax.ShapeDtypeStruct((points, width), f32),
        in_specs=[pl.BlockSpec(memory_space=pltpu.VMEM)] * 2,
        out_specs=pl.BlockSpec(memory_space=pltpu.VMEM),
        scratch_shapes=[
            pltpu.VMEM((n_row, points, width + 2 * rank), f32),
            pltpu.VMEM((n_core * n_col, points, width + 2 * rank), f32),
            pltpu.VMEM((n_row, points, width), f32),
            pltpu.VMEM((n_row, points, width), f32),
            dma((n_row, pieces)),
            dma((n_row, pieces)),
            dma((n_col, pieces)),
            dma((n_col, pieces)),
            dma((n_col, 1)),
            dma((n_col, 1)),
            dma((n_row,)),
            dma((n_row,)),
        ],
        compiler_params=pltpu.CompilerParams(
            collective_id=0, has_side_effects=True, vmem_limit_bytes=48 * 2**20
        ),
    )(jnp.concatenate([features, probe_u, solve_v], axis=1), inv_scale)


def solution(mesh):
    rows, cols = mesh.shape["row"], mesh.shape["col"]
    n_core = 2 if rows % 2 == 0 else 1
    chips = rows // n_core
    n_a, n_b = split(chips), split(cols)
    sizes = (n_core, n_a, n_b, chips // n_a, cols // n_b)
    return jax.shard_map(
        functools.partial(on_device, sizes),
        mesh=mesh,
        in_specs=(P(("row", "col"), None), P(), P(("row", "col"), None), P(("row", "col"), None)),
        out_specs=P(("row", "col"), None),
        check_vma=False,
    )
```

```python
import functools
import math

import jax
import jax.numpy as jnp
from jax import lax
from jax.experimental import pallas as pl
from jax.experimental.pallas import tpu as pltpu
from jax.sharding import PartitionSpec as P

MESH = pl.DeviceIdType.MESH
LAST = (((1,), (1,)), ((), ()))
FIRST = (((1,), (0,)), ((), ()))


def split(count):
    return max(part for part in range(1, math.isqrt(count) + 1) if count % part == 0)


def dot(left, right, dims):
    return lax.dot_general(left, right, dims, preferred_element_type=jnp.float32)


def halves(value):
    hi = value.astype(jnp.bfloat16)
    return hi, (value - hi.astype(jnp.float32)).astype(jnp.bfloat16)


def ends(square, side):
    lane = lax.broadcasted_iota(jnp.int32, (square.shape[0], 128), 1)
    rest, lanes = -0.5 * square, jnp.where(lane < 6, 1.0, 0.0)
    for index in range(3):
        piece = rest.astype(jnp.bfloat16).astype(jnp.float32)
        lanes = jnp.where(lane == 3 * side + index, piece, lanes)
        rest = rest - piece
    return lanes.astype(jnp.bfloat16)


def kernel(
    sizes,
    x_ref,
    scale_ref,
    u_ref,
    v_ref,
    out_ref,
    block_ref,
    scale_buf,
    u_buf,
    v_buf,
    local_sem,
    row_buf,
    col_buf,
    part,
    landed,
    row_send,
    row_recv,
    col_send,
    col_recv,
    twin_send,
    twin_recv,
    red_send,
    red_recv,
):
    n_core, n_a, n_b, n_c, n_d = sizes
    points, width = out_ref.shape
    rank = (block_ref.shape[1] - width) // 2
    row, col = lax.axis_index("row"), lax.axis_index("col")
    core, chip = lax.rem(row, n_core), lax.div(row, n_core)
    a, c = lax.rem(chip, n_a), lax.div(chip, n_a)
    b, d = lax.rem(col, n_b), lax.div(col, n_b)

    def around(own, count):
        return [own] + [lax.rem(own + step, count) for step in range(1, count)]

    cores, cs = around(core, n_core), [n_a * n_core * at for at in around(c, n_c)]
    rows_at = [n_core * at for at in around(a, n_a)]
    bs, ds = around(b, n_b), [n_b * at for at in around(d, n_d)]

    def device(da=0, db=0, dc=0, dd=0, dcore=0):
        return (cs[dc] + rows_at[da] + cores[dcore], ds[dd] + bs[db])

    order = [(0, 0)] + [(0, j) for j in range(1, n_b)] + [(i, 0) for i in range(1, n_a)]
    early = len(order)
    order += [(i, j) for i in range(1, n_a) for j in range(1, n_b)]

    def row_slot(da, db):
        return order.index((da, db))

    def col_slot(dc, dd):
        return dc * n_d + dd

    n_row, n_col = n_a * n_b, n_c * n_d
    peers = [device(da=i, db=j) for i in range(n_a) for j in range(n_b) if i + j > 0]
    peers += [device(dc=i) for i in range(1, n_c)]
    peers += [device(dd=i) for i in range(1, n_d)]
    peers += [device(dcore=i) for i in range(1, n_core)]
    barrier = pltpu.get_barrier_semaphore()
    for peer in peers:
        pl.semaphore_signal(barrier, inc=1, device_id=peer, device_id_type=MESH)

    loads = [
        pltpu.make_async_copy(x_ref, block_ref.at[:, pl.ds(0, width)], local_sem.at[0]),
        pltpu.make_async_copy(u_ref, u_buf, local_sem.at[1]),
        pltpu.make_async_copy(v_ref, v_buf, local_sem.at[2]),
        pltpu.make_async_copy(scale_ref, scale_buf, local_sem.at[3]),
    ]
    for load in loads:
        load.start()
    for load in loads[:3]:
        load.wait()
    block_ref[:, width:] = jnp.concatenate([u_buf[...], v_buf[...]], axis=1)
    pl.semaphore_wait(barrier, len(peers))

    def remote(src, dst, send, recv, to):
        return pltpu.make_async_remote_copy(
            src_ref=src, dst_ref=dst, send_sem=send, recv_sem=recv, device_id=to, device_id_type=MESH
        )

    pieces = row_send.shape[1]

    def in_pieces(count, src, dst, send, recv, to):
        size = points // count
        cuts = [pl.ds(index * size, size) for index in range(count)]
        return [
            remote(src.at[cut], dst.at[cut], send.at[index], recv.at[index], to)
            for index, cut in enumerate(cuts)
        ]

    def row_copy(i, j, by):
        direct = j == 0
        src = block_ref if direct or i == 0 else row_buf.at[row_slot(0, j)]
        to = device(da=n_a - by) if i else device(db=n_b - by)
        dst, count = row_slot(i, j), 1 if direct else pieces
        return in_pieces(count, src, row_buf.at[dst], row_send.at[dst], row_recv.at[dst], to)

    def col_copy(i, j, by):
        direct = j == 0
        src = block_ref if direct or i == 0 else col_buf.at[col_slot(0, j)]
        to = device(dc=n_c - by) if i else device(dd=n_d - by)
        dst, count = col_slot(i, j), 1 if direct else pieces
        return in_pieces(count, src, col_buf.at[dst], col_send.at[dst], col_recv.at[dst], to)

    def twin_copy(slot):
        src = col_buf.at[slot] if slot else block_ref
        dst = col_buf.at[n_col + slot]
        return in_pieces(1, src, dst, twin_send.at[slot], twin_recv.at[slot], device(dcore=1))

    near = [row_copy(0, j, j) for j in range(1, n_b)]
    far = [col_copy(0, j, j) for j in range(1, n_d)]
    side = [[row_copy(i, j, i) for i in range(1, n_a)] for j in range(n_b)]
    over = [[col_copy(i, j, i) for i in range(1, n_c)] for j in range(n_d)]
    twin = [twin_copy(slot) for slot in range(n_col)] if n_core > 1 else []

    def start(copies):
        for copy in copies:
            copy.start()

    def arrive(copies):
        for copy in copies:
            copy.wait_recv()

    def start_twin(i, j):
        if n_core > 1:
            start(twin[col_slot(i, j)])

    for index in range(pieces):
        start([copy[index] for copy in far + near])
    for copy in over[0] + side[0] + twin[:1]:
        start(copy)
    row_buf[0] = block_ref[...]
    col_buf[0] = block_ref[...]

    for index in range(pieces):
        for j, copy in enumerate(far, 1):
            copy[index].wait_recv()
            start([relay[index] for relay in over[j]])
        for j, copy in enumerate(near, 1):
            copy[index].wait_recv()
            start([relay[index] for relay in side[j]])
    for j in range(1, n_d):
        start_twin(0, j)
    for j in range(n_d):
        for i, copy in enumerate(over[j], 1):
            arrive(copy)
            start_twin(i, j)
    for copy in side[0]:
        arrive(copy)

    loads[3].wait()
    scale = scale_buf[...].reshape(1, width)

    def row_side(first, last):
        rows = row_buf[first:last].reshape((last - first) * points, width + 2 * rank)
        row_x, row_uv = rows[:, :width], rows[:, width:]
        row_sq = jnp.sum(row_x * scale * row_x, axis=1, keepdims=True)
        hi, lo = halves(row_x)
        left = jnp.concatenate([hi, lo, hi, ends(row_sq, 1)], axis=1)
        vu_hi, vu_lo = halves(jnp.concatenate([row_uv[:, rank:], row_uv[:, :rank]], axis=1))
        return row_x, left, jnp.concatenate([vu_hi, vu_lo, vu_hi], axis=1)

    def col_side(core_slot):
        cols = col_buf[core_slot * n_col : (core_slot + 1) * n_col]
        cols = cols.reshape(n_col * points, width + 2 * rank)
        col_x = cols[:, :width]
        col_scaled = col_x * scale
        col_sq = jnp.sum(col_scaled * col_x, axis=1, keepdims=True)
        hi, lo = halves(col_scaled)
        right = jnp.concatenate([hi, hi, lo, ends(col_sq, 0)], axis=1)
        uv_hi, uv_lo = halves(cols[:, width:])
        return halves(col_x), right, jnp.concatenate([uv_hi, uv_hi, uv_lo], axis=1)

    def tile(row_terms, col_terms):
        (_, left, vu_left), ((x_hi, x_lo), right, uv_right) = row_terms, col_terms
        coupling = dot(vu_left, uv_right, LAST) * jnp.exp(dot(left, right, LAST))
        hi, lo = halves(coupling)
        both = dot(jnp.concatenate([hi, lo], axis=0), x_hi, FIRST)
        count = left.shape[0]
        pulled = both[:count] + both[count:] + dot(hi, x_lo, FIRST)
        return coupling, pulled, jnp.sum(coupling, axis=1, keepdims=True)

    def finish(first, last, row_x, pulled, sums):
        part[first:last] = (pulled - sums * row_x).reshape(last - first, points, width)
        for slot in range(max(first, 1), last):
            i, j = order[slot]
            to = device(da=i, db=j)
            copy = remote(
                part.at[slot], landed.at[slot], red_send.at[slot], red_recv.at[slot], to
            )
            copy.start()
            reduces.append(copy)

    reduces = []
    row_terms = row_side(0, early)
    row_x = row_terms[0]
    col_terms = [col_side(0)]
    coupling, pulled, sums = tile(row_terms, col_terms[0])
    place = [lax.broadcasted_iota(jnp.int32, (points, n_col * points), axis) for axis in (0, 1)]
    diagonal = jnp.where(place[0] == place[1], coupling[:points], 0.0)
    diagonal = jnp.sum(diagonal, axis=1, keepdims=True)
    diag_hi, diag_lo = (half.astype(jnp.float32) for half in halves(diagonal))
    own = row_x[:points]
    own_hi, own_lo = (half.astype(jnp.float32) for half in halves(own))
    rest = diagonal * own - diag_hi * own_hi - diag_hi * own_lo - diag_lo * own_hi

    for copy in twin:
        arrive(copy)
    for core_slot in range(1, n_core):
        col_terms.append(col_side(core_slot))
        _, more_pulled, more_sums = tile(row_terms, col_terms[core_slot])
        pulled, sums = pulled + more_pulled, sums + more_sums
    finish(0, early, row_x, pulled, sums)

    if early < n_row:
        for copies in side[1:]:
            for copy in copies:
                arrive(copy)
        row_terms = row_side(early, n_row)
        results = [tile(row_terms, terms) for terms in col_terms]
        finish(
            early,
            n_row,
            row_terms[0],
            sum(result[1] for result in results),
            sum(result[2] for result in results),
        )
    total = part[0] + rest
    for slot, copy in enumerate(reduces, 1):
        copy.wait_recv()
        total = total + landed[slot]
    out_ref[...] = total * scale

    for copies in (near, far, *side, *over, twin):
        for copy in copies:
            for part_copy in copy:
                part_copy.wait_send()
    for copy in reduces:
        copy.wait_send()


def on_device(sizes, features, inv_scale, probe_u, solve_v):
    n_core, n_a, n_b, n_c, n_d = sizes
    points, width = features.shape
    rank = probe_u.shape[1]
    n_row, n_col = n_a * n_b, n_c * n_d
    pieces = 2 if points % 16 == 0 else 1
    f32, dma = jnp.float32, pltpu.SemaphoreType.DMA
    return pl.pallas_call(
        functools.partial(kernel, sizes),
        out_shape=jax.ShapeDtypeStruct((points, width), f32),
        in_specs=[pl.BlockSpec(memory_space=pltpu.HBM)] * 4,
        out_specs=pl.BlockSpec(memory_space=pltpu.VMEM),
        scratch_shapes=[
            pltpu.VMEM((points, width + 2 * rank), f32),
            pltpu.VMEM((width,), f32),
            pltpu.VMEM((points, rank), f32),
            pltpu.VMEM((points, rank), f32),
            dma((4,)),
            pltpu.VMEM((n_row, points, width + 2 * rank), f32),
            pltpu.VMEM((n_core * n_col, points, width + 2 * rank), f32),
            pltpu.VMEM((n_row, points, width), f32),
            pltpu.VMEM((n_row, points, width), f32),
            dma((n_row, pieces)),
            dma((n_row, pieces)),
            dma((n_col, pieces)),
            dma((n_col, pieces)),
            dma((n_col, 1)),
            dma((n_col, 1)),
            dma((n_row,)),
            dma((n_row,)),
        ],
        compiler_params=pltpu.CompilerParams(
            collective_id=0, has_side_effects=True, vmem_limit_bytes=48 * 2**20
        ),
    )(*(pltpu.with_memory_space_constraint(x, pltpu.HBM) for x in (features, inv_scale, probe_u, solve_v)))


def solution(mesh):
    rows, cols = mesh.shape["row"], mesh.shape["col"]
    n_core = 2 if rows % 2 == 0 else 1
    chips = rows // n_core
    n_a, n_b = split(chips), split(cols)
    sizes = (n_core, n_a, n_b, chips // n_a, cols // n_b)
    return jax.shard_map(
        functools.partial(on_device, sizes),
        mesh=mesh,
        in_specs=(P(("row", "col"), None), P(), P(("row", "col"), None), P(("row", "col"), None)),
        out_specs=P(("row", "col"), None),
        check_vma=False,
    )
```

```python
import functools
import math

import jax
import jax.numpy as jnp
from jax import lax
from jax.experimental import pallas as pl
from jax.experimental.pallas import tpu as pltpu
from jax.sharding import PartitionSpec as P

MESH = pl.DeviceIdType.MESH
LAST = (((1,), (1,)), ((), ()))
FIRST = (((1,), (0,)), ((), ()))


def split(count):
    return max(part for part in range(1, math.isqrt(count) + 1) if count % part == 0)


def dot(left, right, dims):
    return lax.dot_general(left, right, dims, preferred_element_type=jnp.float32)


def halves(value):
    hi = value.astype(jnp.bfloat16)
    return hi, (value - hi.astype(jnp.float32)).astype(jnp.bfloat16)


def ends(square, side):
    lane = lax.broadcasted_iota(jnp.int32, (square.shape[0], 128), 1)
    rest, lanes = -0.5 * square, jnp.where(lane < 6, 1.0, 0.0)
    for index in range(3):
        piece = rest.astype(jnp.bfloat16).astype(jnp.float32)
        lanes = jnp.where(lane == 3 * side + index, piece, lanes)
        rest = rest - piece
    return lanes.astype(jnp.bfloat16)


def kernel(
    sizes,
    x_ref,
    scale_ref,
    u_ref,
    v_ref,
    out_ref,
    block_ref,
    scale_buf,
    u_buf,
    v_buf,
    local_sem,
    row_buf,
    col_buf,
    part,
    landed,
    row_send,
    row_recv,
    col_send,
    col_recv,
    twin_send,
    twin_recv,
    red_send,
    red_recv,
):
    n_core, n_a, n_b, n_c, n_d = sizes
    points, width = out_ref.shape
    rank = (block_ref.shape[1] - width) // 2
    row, col = lax.axis_index("row"), lax.axis_index("col")
    core, chip = lax.rem(row, n_core), lax.div(row, n_core)
    a, c = lax.rem(chip, n_a), lax.div(chip, n_a)
    b, d = lax.rem(col, n_b), lax.div(col, n_b)

    def around(own, count):
        return [own] + [lax.rem(own + step, count) for step in range(1, count)]

    cores, cs = around(core, n_core), [n_a * n_core * at for at in around(c, n_c)]
    rows_at = [n_core * at for at in around(a, n_a)]
    bs, ds = around(b, n_b), [n_b * at for at in around(d, n_d)]

    def device(da=0, db=0, dc=0, dd=0, dcore=0):
        return (cs[dc] + rows_at[da] + cores[dcore], ds[dd] + bs[db])

    order = [(0, 0)] + [(0, j) for j in range(1, n_b)] + [(i, 0) for i in range(1, n_a)]
    early = len(order)
    order += [(i, j) for i in range(1, n_a) for j in range(1, n_b)]

    def row_slot(da, db):
        return order.index((da, db))

    def col_slot(dc, dd):
        return dc * n_d + dd

    n_row, n_col = n_a * n_b, n_c * n_d
    peers = [device(da=i, db=j) for i in range(n_a) for j in range(n_b) if i + j > 0]
    peers += [device(dc=i, dd=j) for i in range(n_c) for j in range(n_d) if i + j > 0]
    peers += [device(dcore=i) for i in range(1, n_core)]
    barrier = pltpu.get_barrier_semaphore()
    for peer in peers:
        pl.semaphore_signal(barrier, inc=1, device_id=peer, device_id_type=MESH)

    loads = [
        pltpu.make_async_copy(x_ref, block_ref.at[:, pl.ds(0, width)], local_sem.at[0]),
        pltpu.make_async_copy(u_ref, u_buf, local_sem.at[1]),
        pltpu.make_async_copy(v_ref, v_buf, local_sem.at[2]),
        pltpu.make_async_copy(scale_ref, scale_buf, local_sem.at[3]),
    ]
    for load in loads:
        load.start()
    for load in loads[:3]:
        load.wait()
    block_ref[:, width:] = jnp.concatenate([u_buf[...], v_buf[...]], axis=1)
    pl.semaphore_wait(barrier, len(peers))

    def remote(src, dst, send, recv, to):
        return pltpu.make_async_remote_copy(
            src_ref=src, dst_ref=dst, send_sem=send, recv_sem=recv, device_id=to, device_id_type=MESH
        )

    pieces = row_send.shape[1]

    def in_pieces(count, src, dst, send, recv, to):
        size = points // count
        cuts = [pl.ds(index * size, size) for index in range(count)]
        return [
            remote(src.at[cut], dst.at[cut], send.at[index], recv.at[index], to)
            for index, cut in enumerate(cuts)
        ]

    def row_copy(i, j, by):
        direct = j == 0
        src = block_ref if direct or i == 0 else row_buf.at[row_slot(0, j)]
        to = device(da=n_a - by) if i else device(db=n_b - by)
        dst, count = row_slot(i, j), 1 if direct else pieces
        return in_pieces(count, src, row_buf.at[dst], row_send.at[dst], row_recv.at[dst], to)

    def col_copy(i, j):
        dst, to = col_slot(i, j), device(dc=(n_c - i) % n_c, dd=(n_d - j) % n_d)
        return remote(block_ref, col_buf.at[dst], col_send.at[dst], col_recv.at[dst], to)

    def twin_copy(slot):
        src = col_buf.at[slot] if slot else block_ref
        dst = col_buf.at[n_col + slot]
        return in_pieces(1, src, dst, twin_send.at[slot], twin_recv.at[slot], device(dcore=1))

    near = [row_copy(0, j, j) for j in range(1, n_b)]
    side = [[row_copy(i, j, i) for i in range(1, n_a)] for j in range(n_b)]
    cols = [(i, j) for i in range(n_c) for j in range(n_d) if i + j > 0]
    over = {(i, j): col_copy(i, j) for i, j in cols}
    twin = [twin_copy(slot) for slot in range(n_col)] if n_core > 1 else []

    def start(copies):
        for copy in copies:
            copy.start()

    def arrive(copies):
        for copy in copies:
            copy.wait_recv()

    def start_twin(i, j):
        if n_core > 1:
            start(twin[col_slot(i, j)])

    apart = [at for at in cols if 0 not in at]
    direct = [at for at in cols if 0 in at]
    start([over[at] for at in apart])
    for index in range(pieces):
        start([copy[index] for copy in near])
    start([over[at] for at in direct])
    for copy in side[0] + twin[:1]:
        start(copy)
    row_buf[0] = block_ref[...]
    col_buf[0] = block_ref[...]

    for index in range(pieces):
        for j, copy in enumerate(near, 1):
            copy[index].wait_recv()
            start([relay[index] for relay in side[j]])
    for at in direct + apart:
        over[at].wait_recv()
        start_twin(*at)
    for copy in side[0]:
        arrive(copy)

    loads[3].wait()
    scale = scale_buf[...].reshape(1, width)

    def row_side(first, last):
        rows = row_buf[first:last].reshape((last - first) * points, width + 2 * rank)
        row_x, row_uv = rows[:, :width], rows[:, width:]
        row_sq = jnp.sum(row_x * scale * row_x, axis=1, keepdims=True)
        hi, lo = halves(row_x)
        left = jnp.concatenate([hi, lo, hi, ends(row_sq, 1)], axis=1)
        vu_hi, vu_lo = halves(jnp.concatenate([row_uv[:, rank:], row_uv[:, :rank]], axis=1))
        return row_x, left, jnp.concatenate([vu_hi, vu_lo, vu_hi], axis=1)

    def col_side(core_slot):
        cols = col_buf[core_slot * n_col : (core_slot + 1) * n_col]
        cols = cols.reshape(n_col * points, width + 2 * rank)
        col_x = cols[:, :width]
        col_scaled = col_x * scale
        col_sq = jnp.sum(col_scaled * col_x, axis=1, keepdims=True)
        hi, lo = halves(col_scaled)
        right = jnp.concatenate([hi, hi, lo, ends(col_sq, 0)], axis=1)
        uv_hi, uv_lo = halves(cols[:, width:])
        return halves(col_x), right, jnp.concatenate([uv_hi, uv_hi, uv_lo], axis=1)

    def tile(row_terms, col_terms):
        (_, left, vu_left), ((x_hi, x_lo), right, uv_right) = row_terms, col_terms
        coupling = dot(vu_left, uv_right, LAST) * jnp.exp(dot(left, right, LAST))
        hi, lo = halves(coupling)
        both = dot(jnp.concatenate([hi, lo], axis=0), x_hi, FIRST)
        count = left.shape[0]
        pulled = both[:count] + both[count:] + dot(hi, x_lo, FIRST)
        return coupling, pulled, jnp.sum(coupling, axis=1, keepdims=True)

    def finish(first, last, row_x, pulled, sums):
        part[first:last] = (pulled - sums * row_x).reshape(last - first, points, width)
        for slot in range(max(first, 1), last):
            i, j = order[slot]
            to = device(da=i, db=j)
            copy = remote(
                part.at[slot], landed.at[slot], red_send.at[slot], red_recv.at[slot], to
            )
            copy.start()
            reduces.append(copy)

    reduces = []
    row_terms = row_side(0, early)
    row_x = row_terms[0]
    col_terms = [col_side(0)]
    coupling, pulled, sums = tile(row_terms, col_terms[0])
    place = [lax.broadcasted_iota(jnp.int32, (points, n_col * points), axis) for axis in (0, 1)]
    diagonal = jnp.where(place[0] == place[1], coupling[:points], 0.0)
    diagonal = jnp.sum(diagonal, axis=1, keepdims=True)
    diag_hi, diag_lo = (half.astype(jnp.float32) for half in halves(diagonal))
    own = row_x[:points]
    own_hi, own_lo = (half.astype(jnp.float32) for half in halves(own))
    rest = diagonal * own - diag_hi * own_hi - diag_hi * own_lo - diag_lo * own_hi

    for copy in twin:
        arrive(copy)
    for core_slot in range(1, n_core):
        col_terms.append(col_side(core_slot))
        _, more_pulled, more_sums = tile(row_terms, col_terms[core_slot])
        pulled, sums = pulled + more_pulled, sums + more_sums
    finish(0, early, row_x, pulled, sums)

    if early < n_row:
        for copies in side[1:]:
            for copy in copies:
                arrive(copy)
        row_terms = row_side(early, n_row)
        results = [tile(row_terms, terms) for terms in col_terms]
        finish(
            early,
            n_row,
            row_terms[0],
            sum(result[1] for result in results),
            sum(result[2] for result in results),
        )
    total = part[0] + rest
    for slot, copy in enumerate(reduces, 1):
        copy.wait_recv()
        total = total + landed[slot]
    out_ref[...] = total * scale

    for copies in (near, *side, twin):
        for copy in copies:
            for part_copy in copy:
                part_copy.wait_send()
    for copy in over.values():
        copy.wait_send()
    for copy in reduces:
        copy.wait_send()


def on_device(sizes, features, inv_scale, probe_u, solve_v):
    n_core, n_a, n_b, n_c, n_d = sizes
    points, width = features.shape
    rank = probe_u.shape[1]
    n_row, n_col = n_a * n_b, n_c * n_d
    pieces = 2 if points % 16 == 0 else 1
    f32, dma = jnp.float32, pltpu.SemaphoreType.DMA
    return pl.pallas_call(
        functools.partial(kernel, sizes),
        out_shape=jax.ShapeDtypeStruct((points, width), f32),
        in_specs=[pl.BlockSpec(memory_space=pltpu.HBM)] * 4,
        out_specs=pl.BlockSpec(memory_space=pltpu.VMEM),
        scratch_shapes=[
            pltpu.VMEM((points, width + 2 * rank), f32),
            pltpu.VMEM((width,), f32),
            pltpu.VMEM((points, rank), f32),
            pltpu.VMEM((points, rank), f32),
            dma((4,)),
            pltpu.VMEM((n_row, points, width + 2 * rank), f32),
            pltpu.VMEM((n_core * n_col, points, width + 2 * rank), f32),
            pltpu.VMEM((n_row, points, width), f32),
            pltpu.VMEM((n_row, points, width), f32),
            dma((n_row, pieces)),
            dma((n_row, pieces)),
            dma((n_col,)),
            dma((n_col,)),
            dma((n_col, 1)),
            dma((n_col, 1)),
            dma((n_row,)),
            dma((n_row,)),
        ],
        compiler_params=pltpu.CompilerParams(
            collective_id=0, has_side_effects=True, vmem_limit_bytes=48 * 2**20
        ),
    )(*(pltpu.with_memory_space_constraint(x, pltpu.HBM) for x in (features, inv_scale, probe_u, solve_v)))


def solution(mesh):
    rows, cols = mesh.shape["row"], mesh.shape["col"]
    n_core = 2 if rows % 2 == 0 else 1
    chips = rows // n_core
    n_a, n_b = split(chips), split(cols)
    sizes = (n_core, n_a, n_b, chips // n_a, cols // n_b)
    return jax.shard_map(
        functools.partial(on_device, sizes),
        mesh=mesh,
        in_specs=(P(("row", "col"), None), P(), P(("row", "col"), None), P(("row", "col"), None)),
        out_specs=P(("row", "col"), None),
        check_vma=False,
    )
```
